512 devices in a mesh: grp: 4 (over y_hi, core), seq: 16 (over z), kv: 8 (over x, y_lo).
Axes of the slice: x: 4, y: 4 (y_hi: 2, y_lo: 2; y = y_hi * 2 + y_lo), z: 16, core: 2. Of those that a mesh axis runs over, the one named last changes fastest.
Arguments:
- queries: bfloat16 [16384, 8192], P(('grp', 'seq'), 'kv'), parts along dimension 0, may hold values from -4.5 to 4.5
- resp_keys: bfloat16 [16384, 1024], P(('grp', 'seq'), 'kv'), parts along dimension 0, may hold values from -4.5 to 4.5
- resp_values: bfloat16 [16384, 1024], P(('grp', 'seq'), 'kv'), parts along dimension 0, may hold values from -4.5 to 4.5
- prompt_keys: bfloat16 [8192, 1024], P(('grp', 'seq'), 'kv'), parts along dimension 0, may hold values from -4.5 to 4.5
- prompt_values: bfloat16 [8192, 1024], P(('grp', 'seq'), 'kv'), parts along dimension 0, may hold values from -4.5 to 4.5
- outputs: bfloat16 [16384, 8192], P(('grp', 'seq'), 'kv'), parts along dimension 0, may hold values from -5 to 5
- out_grads: bfloat16 [16384, 8192], P(('grp', 'seq'), 'kv'), parts along dimension 0, may hold values from -24 to 24
- lengths: int32 [64], P(('grp', 'seq')), parts along dimension 0, may hold values from 1 to 256, 2048 in all
Outputs:
- query_grads: bfloat16 [16384, 8192], P(('grp', 'seq'), 'kv'), parts along dimension 0
- resp_key_grads: bfloat16 [16384, 1024], P(('grp', 'seq'), 'kv'), parts along dimension 0
- resp_value_grads: bfloat16 [16384, 1024], P(('grp', 'seq'), 'kv'), parts along dimension 0
- prompt_key_grads: bfloat16 [8192, 1024], P(('grp', 'seq'), 'kv'), parts along dimension 0
- prompt_value_grads: bfloat16 [8192, 1024], P(('grp', 'seq'), 'kv'), parts along dimension 0
The draws below stay inside these ranges and needn't reach their ends.
There are 4 independent parts, one for each index of `grp`. The reference program is written for one: setup_inputs(seed, part) draws one part's arguments, and reference() takes and returns one part's arrays. A program takes and returns all parts, laid end to end along the dimension named above; each array names one. Nothing has to cross between parts.
Inputs may be any that keep to these rules, and one draw needn't show every extreme that they name: `lengths`: some response of each group has exactly 256 live tokens.
All inputs are finite; a program needn't handle non-finite values.
Results may differ from the reference program's by a relative error of at most 0.025.
Values may be sent and summed in bfloat16 or wider, within the bound.
A program may use at most 64 MiB of HBM per device.

```python
import math
import jax
import jax.numpy as jnp
import numpy as np
from jax import lax

HD = 128
GQ = 8
R = 256
KVH = 8
HQ = 64
SEQS = 16
P_SIZE = 2048


def draw_queries(key, part):
    key = jax.random.fold_in(key, 11)
    shape = (SEQS * R, GQ * KVH * HD)
    result = jnp.clip(jax.random.normal(key, shape, jnp.float32), -4.5, 4.5)
    return result.astype(jnp.bfloat16)


def draw_prompt_keys(key, part):
    key = jax.random.fold_in(key, 12)
    shape = (P_SIZE, KVH * HD)
    result = jnp.clip(jax.random.normal(key, shape, jnp.float32), -4.5, 4.5)
    return result.astype(jnp.bfloat16)


def block_levels(stream_key, shape, shards, smallest, top_value):
    def one(axis_at, shards_of):
        draws = jax.random.uniform(jax.random.fold_in(jax.random.fold_in(stream_key, 6), axis_at), (shards_of,), jnp.float32, smallest / len(shards), top_value / len(shards))
        return jnp.repeat(jnp.exp(draws), shape[axis_at] // shards_of).reshape((-1,) + (1,) * (len(shape) - axis_at - 1))

    level = one(*shards[0])
    for cut in shards[1:]:
        level = level * one(*cut)
    return level


def profile(number_of, total, most, slope):
    weights = [(1 << 20) // math.isqrt(standing ** slope) + 1 for standing in range(2, number_of + 1)]
    spare, holding = total - most - (number_of - 1), [1] * (number_of - 1)
    while spare > 0:
        candidates = [i for i in range(number_of - 1) if holding[i] < most]
        mass, budget = sum([weights[i] for i in candidates]), spare
        for i in candidates:
            more = min(most - holding[i], max(1, budget * weights[i] // mass), spare)
            holding[i] = holding[i] + more
            spare = spare - more
    return np.array([most] + holding)


def uneven(own_key, count, total, most, skew):
    if count == 2:
        one = jax.random.randint(own_key, (), max(1, total - most), min(most, total - 1) + 1)
        return jnp.stack([one, total - one])
    sizes = jnp.asarray(profile(count, total, most, skew), jnp.int32)
    couples = (count - 1) // 2
    donor, receiver = sizes[1:1 + 2 * couples:2], sizes[2:2 + 2 * couples:2]
    slack = jnp.minimum(donor - 1, most - receiver)
    moved = jax.random.randint(jax.random.fold_in(own_key, 1), (couples,), 0, 1 << 20) % (slack + 1)
    sizes = sizes.at[1:1 + 2 * couples:2].set(donor - moved).at[2:2 + 2 * couples:2].set(receiver + moved)
    return sizes[jax.random.permutation(jax.random.fold_in(own_key, 2), count)]


def noise(rng, extent, width, most, shards=(), kind=jnp.bfloat16):
    entries = jax.random.normal(rng, extent, jnp.float32) * width
    if len(shards) > 0:
        entries = block_levels(rng, extent, shards, -0.22, 0.18) * entries
    return jnp.clip(entries, min=-most, max=most).astype(kind)


def setup_inputs(seed: int = 0, part: int = 0) -> dict:
    key_list = jax.random.split(jax.random.key(seed), 9)
    part_keys = jax.random.split(jax.random.fold_in(key_list[8], part), 9)
    return {
        "queries": draw_queries(jax.random.fold_in(jax.random.fold_in(key_list[8], part), 71), part),
        "resp_keys": noise(part_keys[1], (SEQS * R, KVH * HD), 1.0, 4.5, ((0, 16), (1, 8))),
        "resp_values": noise(part_keys[2], (SEQS * R, KVH * HD), 1.0, 4.5, ((0, 16), (1, 8))),
        "prompt_keys": draw_prompt_keys(jax.random.fold_in(jax.random.fold_in(key_list[8], part), 71), part),
        "prompt_values": noise(part_keys[4], (P_SIZE, KVH * HD), 1.0, 4.5, ((0, 16), (1, 8))),
        "outputs": noise(part_keys[5], (SEQS * R, HQ * HD), 1.0, 5.0, ((0, 16), (1, 8))),
        "out_grads": noise(part_keys[6], (SEQS * R, HQ * HD), 4.0, 24.0, ((0, 16), (1, 8))),
        "lengths": uneven(part_keys[7], SEQS, R * SEQS // 2, R, 1).astype(jnp.int32),
    }


def response_grads(query_blk, key_resp, value_resp, key_prompt, value_prompt, out_blk, grad_blk, length):
    rows = query_blk.shape[0]
    prompt_rows = key_prompt.shape[0]
    head_dim = key_resp.shape[1]
    scale = head_dim ** -0.5
    keys = jnp.concatenate([key_prompt, key_resp], 0).astype(jnp.float32)
    values = jnp.concatenate([value_prompt, value_resp], 0).astype(jnp.float32)
    row_pos = jnp.arange(rows, dtype=jnp.int32)
    key_pos = jnp.arange(keys.shape[0], dtype=jnp.int32) - prompt_rows
    allowed = key_pos[None, :] <= row_pos[:, None]
    live = row_pos < length
    masked = jnp.where(live[:, None, None], grad_blk, jnp.zeros_like(grad_blk))
    query_f = query_blk.astype(jnp.float32)
    grad_f = masked.astype(jnp.float32)
    scores = jnp.einsum("rhd,kd->hrk", query_f, keys) * scale
    scores = jnp.where(allowed[None], scores, -jnp.inf)
    lse = jax.nn.logsumexp(scores, axis=2, keepdims=True)
    probs = jnp.exp(scores - lse)
    dprob = jnp.einsum("rhd,kd->hrk", grad_f, values)
    delta = jnp.einsum("rhd,rhd->hr", grad_f, out_blk.astype(jnp.float32))
    dscore = lax.optimization_barrier((probs * (dprob - delta[:, :, None]) * scale).astype(jnp.bfloat16)).astype(jnp.float32)
    probs_rounded = lax.optimization_barrier(probs.astype(jnp.bfloat16)).astype(jnp.float32)
    dquery = jnp.einsum("hrk,kd->rhd", dscore, keys)
    dkeys = jnp.einsum("hrk,rhd->kd", dscore, query_f)
    dvalues = jnp.einsum("hrk,rhd->kd", probs_rounded, grad_f)
    return dquery, dkeys, dvalues


def reference(queries, resp_keys, resp_values, prompt_keys, prompt_values, outputs, out_grads, lengths):
    query5 = queries.reshape(SEQS, R, KVH, GQ, HD).transpose(2, 0, 1, 3, 4)
    out5 = outputs.reshape(SEQS, R, KVH, GQ, HD).transpose(2, 0, 1, 3, 4)
    grad5 = out_grads.reshape(SEQS, R, KVH, GQ, HD).transpose(2, 0, 1, 3, 4)
    key4 = resp_keys.reshape(SEQS, R, KVH, HD).transpose(2, 0, 1, 3)
    value4 = resp_values.reshape(SEQS, R, KVH, HD).transpose(2, 0, 1, 3)
    pkey3 = prompt_keys.reshape(P_SIZE, KVH, HD).transpose(1, 0, 2)
    pvalue3 = prompt_values.reshape(P_SIZE, KVH, HD).transpose(1, 0, 2)

    def per_head(items):
        query_h, key_h, value_h, pkey_h, pvalue_h, out_h, grad_h = items

        def per_response(carry, inner):
            query_s, key_s, value_s, out_s, grad_s, length = inner
            dquery, dkeys, dvalues = response_grads(query_s, key_s, value_s, pkey_h, pvalue_h, out_s, grad_s, length)
            key_part = lax.optimization_barrier(dkeys[:P_SIZE].astype(jnp.bfloat16)).astype(jnp.float32)
            value_part = lax.optimization_barrier(dvalues[:P_SIZE].astype(jnp.bfloat16)).astype(jnp.float32)
            carry = (carry[0] + key_part, carry[1] + value_part)
            return carry, (dquery.astype(jnp.bfloat16), dkeys[P_SIZE:].astype(jnp.bfloat16), dvalues[P_SIZE:].astype(jnp.bfloat16))

        start = (jnp.zeros((P_SIZE, HD), jnp.float32), jnp.zeros((P_SIZE, HD), jnp.float32))
        sums, stacked = lax.scan(per_response, start, (query_h, key_h, value_h, out_h, grad_h, lengths))
        return stacked[0], stacked[1], stacked[2], sums[0].astype(jnp.bfloat16), sums[1].astype(jnp.bfloat16)

    dquery, dkey_resp, dvalue_resp, dkey_prompt, dvalue_prompt = lax.map(per_head, (query5, key4, value4, pkey3, pvalue3, out5, grad5))
    query_grads = dquery.transpose(1, 2, 0, 3, 4).reshape(SEQS * R, HQ * HD)
    resp_key_grads = dkey_resp.transpose(1, 2, 0, 3).reshape(SEQS * R, KVH * HD)
    resp_value_grads = dvalue_resp.transpose(1, 2, 0, 3).reshape(SEQS * R, KVH * HD)
    prompt_key_grads = dkey_prompt.transpose(1, 0, 2).reshape(P_SIZE, KVH * HD)
    prompt_value_grads = dvalue_prompt.transpose(1, 0, 2).reshape(P_SIZE, KVH * HD)
    return query_grads, resp_key_grads, resp_value_grads, prompt_key_grads, prompt_value_grads
```

```python
import functools

import jax
import jax.numpy as jnp
from jax import lax
from jax.experimental import pallas as pl
from jax.experimental.pallas import tpu as pltpu
from jax.sharding import PartitionSpec as P

MESH = pl.DeviceIdType.MESH
F32 = jnp.float32
BF16 = jnp.bfloat16
LOG2E = 1.4426950408889634
LOW = -1e30
PARENT = {1: 0, 2: 0, 3: 2, 4: 2, 5: 4, 6: 4, 7: 6, 8: 6}
HU = 2


def dot(a, b):
    return jnp.dot(a, b, preferred_element_type=F32)


def split3(x):
    hi = x.astype(BF16).astype(F32)
    mid = (x - hi).astype(BF16).astype(F32)
    lo = ((x - hi) - mid).astype(BF16).astype(F32)
    row = lax.broadcasted_iota(jnp.int32, (16, x.shape[1]), 0)
    out = jnp.where(row == 0, hi, jnp.where(row == 1, mid, jnp.where(row == 2, lo, 0.0)))
    return out.astype(BF16)


def kernel(
    n, heads, scale,
    q_hbm, kr_hbm, vr_hbm, kp_hbm, vp_hbm, o_hbm, g_hbm, len_ref,
    dq_hbm, dkr_hbm, dvr_hbm, dkp_hbm, dvp_hbm,
    kv, q3, g3, o3, qt, gt, kt, ds, part, sums, got, dq3, resp_out, prompt_out, ext, m8, l8,
    ag_send, ag_recv, rs_send, rs_recv, in_sem, kv_sem, out_sem,
):
    c2 = scale * LOG2E
    rows = q3.shape[1]
    head_dim = q3.shape[2]
    chunk = 2 * head_dim
    me = lax.axis_index("seq")

    def at(step):
        return {"seq": lax.rem(me + step + n, n)}

    barrier = pltpu.get_barrier_semaphore()
    for step in (1, -1, 2, -2):
        pl.semaphore_signal(barrier, inc=1, device_id=at(step), device_id_type=MESH)

    own = 8 * chunk
    local = [
        pltpu.make_async_copy(kp_hbm, kv.at[0, pl.ds(own, 128)], kv_sem.at[0]),
        pltpu.make_async_copy(vp_hbm, kv.at[1, pl.ds(own, 128)], kv_sem.at[1]),
        pltpu.make_async_copy(kr_hbm, kv.at[0, pl.ds(0, chunk)], kv_sem.at[2]),
        pltpu.make_async_copy(vr_hbm, kv.at[1, pl.ds(0, chunk)], kv_sem.at[3]),
    ]
    for copy in local:
        copy.start()
    loads = []
    for h in range(heads):
        for a, (src, dst) in enumerate(((q_hbm, q3), (g_hbm, g3), (o_hbm, o3))):
            copy = pltpu.make_async_copy(
                src.at[:, pl.ds(h * head_dim, head_dim)], dst.at[h], in_sem.at[a, h]
            )
            copy.start()
            loads.append(copy)

    def slot(d, way):
        if d == 8:
            return pl.ds(own + 128 + 64 * way, 64)
        return pl.ds(d * chunk + 128 * way, 128)

    def gather(kind, d, way):
        pa = PARENT[d]
        step = (d - pa) * (1 if way == 0 else -1)
        if pa == 0:
            src = (kp_hbm, vp_hbm)[kind]
        elif d == 8:
            src = kv.at[kind, pl.ds(pa * chunk + 128 * way + 64 * way, 64)]
        else:
            src = kv.at[kind, slot(pa, way)]
        return pltpu.make_async_remote_copy(
            src_ref=src, dst_ref=kv.at[kind, slot(d, way)],
            send_sem=ag_send.at[kind, way, d - 1], recv_sem=ag_recv.at[kind, way, d - 1],
            device_id=at(step), device_id_type=MESH,
        )

    ag = {(k, d, w): gather(k, d, w) for k in range(2) for d in range(1, 9) for w in range(2)}

    pl.semaphore_wait(barrier, 4)
    for kind in range(2):
        for d in (2, 1):
            for way in range(2):
                ag[kind, d, way].start()

    lane = lax.broadcasted_iota(jnp.int32, (chunk, 128), 1)
    ext[...] = jnp.where(lane < 3, -1.0, 0.0).astype(BF16)
    qt[pl.ds(head_dim, 128), :] = jnp.zeros((128, qt.shape[1]), BF16)
    gt[pl.ds(head_dim, 128), :] = jnp.zeros((128, gt.shape[1]), BF16)
    m8[...] = jnp.full(m8.shape, LOW, F32)
    l8[...] = jnp.zeros(l8.shape, F32)
    for copy in loads:
        copy.wait()
    length = len_ref[0]
    live = lax.broadcasted_iota(jnp.int32, (rows, head_dim), 0) < length

    def cols(h):
        return pl.ds(pl.multiple_of(h * rows, rows), rows)

    def prepare(h, carry):
        q = q3[h].astype(F32)
        g = jnp.where(live, g3[h].astype(F32), 0.0)
        o = o3[h].astype(F32)
        g3[h] = g.astype(BF16)
        g_t = g.T
        delta = jnp.sum(g_t * o.T, axis=0, keepdims=True)
        qt[pl.ds(0, head_dim), cols(h)] = q.T.astype(BF16)
        gt[pl.ds(0, head_dim), cols(h)] = g_t.astype(BF16)
        gt[pl.ds(head_dim, 16), cols(h)] = split3(delta)
        return carry

    lax.fori_loop(0, heads, prepare, 0)

    def causal():
        key = lax.broadcasted_iota(jnp.int32, (chunk, rows), 0)
        token = lax.broadcasted_iota(jnp.int32, (chunk, rows), 1)
        return key <= token

    def chunk_rows(c):
        if isinstance(c, int):
            return pl.ds(c * chunk, chunk)
        return pl.ds(pl.multiple_of(c * chunk, chunk), chunk)

    def first_pass(c, masked=False):
        keys = kv[0, chunk_rows(c)]
        kt[:, chunk_rows(c)] = keys.astype(F32).T.astype(BF16)

        def step(h, carry):
            s = dot(keys, qt[pl.ds(0, head_dim), cols(h)])
            if masked:
                s = jnp.where(causal(), s, LOW)
            s = s.reshape(chunk // 8, 8, rows)
            old = m8[h]
            new = jnp.maximum(old, jnp.max(s, axis=0))
            e = jnp.exp2((s - new[None]) * c2)
            l8[h] = l8[h] * jnp.exp2((old - new) * c2) + jnp.sum(e, axis=0)
            m8[h] = new
            return carry

        lax.fori_loop(0, heads, step, 0, unroll=HU)

    def finish_first():
        def step(h, carry):
            m = jnp.max(m8[h], axis=0, keepdims=True)
            total = jnp.sum(l8[h] * jnp.exp2((m8[h] - m) * c2), axis=0, keepdims=True)
            lse = m + jnp.log(total) * (1.0 / scale)
            qt[pl.ds(head_dim, 16), cols(h)] = split3(lse)
            return carry

        lax.fori_loop(0, heads, step, 0, unroll=HU)

    def second_pass(c, masked=False):
        keys = jnp.concatenate([kv[0, chunk_rows(c)], ext[...]], axis=1)
        values = jnp.concatenate([kv[1, chunk_rows(c)], ext[...]], axis=1)
        zero = jnp.zeros((chunk, head_dim), F32)
        part[0, chunk_rows(c)] = zero
        part[1, chunk_rows(c)] = zero

        def step(h, carry):
            p = jnp.exp2(dot(keys, qt[:, cols(h)]) * c2)
            if masked:
                p = jnp.where(causal(), p, 0.0)
            dp = dot(values, gt[:, cols(h)])
            d_s = (p * dp).astype(BF16)
            ds[chunk_rows(c), cols(h)] = d_s
            part[1, chunk_rows(c)] += dot(p.astype(BF16), g3[h])
            part[0, chunk_rows(c)] += dot(d_s, q3[h])
            return carry

        lax.fori_loop(0, heads, step, 0, unroll=HU)

    local[2].wait()
    local[3].wait()
    first_pass(0, masked=True)
    local[0].wait()
    local[1].wait()

    def pair(hi, body):
        def step(i, carry):
            body(hi - i)
            return carry

        lax.fori_loop(0, 2, step, 0)

    for stage in (1, 2, 3, 4):
        if stage < 4:
            for kind in range(2):
                for way in range(2):
                    ag[kind, 2 * stage, way].wait_recv()
                    ag[kind, 2 * stage + 2, way].start()
                    ag[kind, 2 * stage + 1, way].start()
            for kind in range(2):
                for way in range(2):
                    ag[kind, 2 * stage - 1, way].wait_recv()
        else:
            for kind in range(2):
                for d in (8, 7):
                    for way in range(2):
                        ag[kind, d, way].wait_recv()
        pair(2 * stage, first_pass)
    finish_first()

    factor = (scale, 1.0)

    def mine(kind, d, way):
        if d == 0:
            r = pl.ds(own, 128)
        elif d == 8:
            r = pl.ds(own + 128 + 64 * way, 64)
        else:
            r = pl.ds(d * chunk + 128 * (1 - way), 128)
        return part[kind, r] * factor[kind]

    def rs_rows(d, way):
        return pl.ds(64 * way, 64) if d == 8 else pl.ds(0, 128)

    def scatter(kind, d, way):
        step = (d - PARENT[d]) * (1 if way == 0 else -1)
        r = rs_rows(d, way)
        return pltpu.make_async_remote_copy(
            src_ref=sums.at[kind, way, d - 1, r], dst_ref=got.at[kind, way, d - 1, r],
            send_sem=rs_send.at[kind, way, d - 1], recv_sem=rs_recv.at[kind, way, d - 1],
            device_id=at(step), device_id_type=MESH,
        )

    rs = {(k, d, w): scatter(k, d, w) for k in range(2) for d in range(1, 9) for w in range(2)}

    def total(kind, d, way, acc):
        for child in (8, 7, 6, 5, 4, 3, 2, 1):
            if PARENT[child] != d:
                continue
            rs[kind, child, way].wait_recv()
            term = got[kind, way, child - 1, rs_rows(child, way)].astype(F32)
            if child == 8:
                if way == 0:
                    acc = jnp.concatenate([acc[:64] + term, acc[64:]], axis=0)
                else:
                    acc = jnp.concatenate([acc[:64], acc[64:] + term], axis=0)
            else:
                acc = acc + term
        return acc

    def send_sum(kind, d, way):
        acc = total(kind, d, way, mine(kind, d, way))
        sums[kind, way, d - 1, rs_rows(d, way)] = acc.astype(BF16)
        rs[kind, d, way].start()

    for stage in (4, 3, 2, 1):
        pair(2 * stage, second_pass)
        for d in (2 * stage - 1, 2 * stage):
            for kind in (1, 0):
                for way in range(2):
                    send_sum(kind, d, way)

    second_pass(0, masked=True)
    resp_out[0] = (part[0, pl.ds(0, chunk)] * scale).astype(BF16)
    resp_out[1] = part[1, pl.ds(0, chunk)].astype(BF16)
    outs = [
        pltpu.make_async_copy(resp_out.at[0], dkr_hbm, kv_sem.at[0]),
        pltpu.make_async_copy(resp_out.at[1], dvr_hbm, kv_sem.at[1]),
    ]
    for copy in outs:
        copy.start()

    def query_grad(h, carry):
        d_q = dot(kt[...], ds[:, cols(h)]) * scale
        dq3[h] = d_q.T.astype(BF16)
        return carry

    lax.fori_loop(0, heads, query_grad, 0, unroll=HU)
    for h in range(heads):
        copy = pltpu.make_async_copy(
            dq3.at[h], dq_hbm.at[:, pl.ds(h * head_dim, head_dim)], out_sem.at[h]
        )
        copy.start()
        outs.append(copy)

    for kind in (1, 0):
        acc = mine(kind, 0, 0)
        for way in range(2):
            acc = total(kind, 0, way, acc)
        prompt_out[kind] = acc.astype(BF16)
        copy = pltpu.make_async_copy(
            prompt_out.at[kind], (dkp_hbm, dvp_hbm)[kind], kv_sem.at[2 + kind]
        )
        copy.start()
        outs.append(copy)

    for copy in ag.values():
        copy.wait_send()
    for copy in rs.values():
        copy.wait_send()
    for copy in outs:
        copy.wait()


def per_device(n, queries, resp_keys, resp_values, prompt_keys, prompt_values, outputs, out_grads, lengths):
    rows = queries.shape[0]
    head_dim = resp_keys.shape[1]
    heads = queries.shape[1] // head_dim
    scale = head_dim ** (-0.5)
    keys = n * prompt_keys.shape[0] + rows
    wide = heads * rows
    any_spec = pl.BlockSpec(memory_space=pl.ANY)
    shape = jax.ShapeDtypeStruct
    return pl.pallas_call(
        functools.partial(kernel, n, heads, scale),
        out_shape=(
            shape(queries.shape, BF16),
            shape(resp_keys.shape, BF16),
            shape(resp_values.shape, BF16),
            shape(prompt_keys.shape, BF16),
            shape(prompt_values.shape, BF16),
        ),
        in_specs=[any_spec] * 7 + [pl.BlockSpec(memory_space=pltpu.SMEM)],
        out_specs=(any_spec,) * 5,
        scratch_shapes=[
            pltpu.VMEM((2, keys, head_dim), BF16),
            pltpu.VMEM((heads, rows, head_dim), BF16),
            pltpu.VMEM((heads, rows, head_dim), BF16),
            pltpu.VMEM((heads, rows, head_dim), BF16),
            pltpu.VMEM((2 * head_dim, wide), BF16),
            pltpu.VMEM((2 * head_dim, wide), BF16),
            pltpu.VMEM((head_dim, keys), BF16),
            pltpu.VMEM((keys, wide), BF16),
            pltpu.VMEM((2, keys, head_dim), F32),
            pltpu.VMEM((2, 2, 8, 128, head_dim), BF16),
            pltpu.VMEM((2, 2, 8, 128, head_dim), BF16),
            pltpu.VMEM((heads, rows, head_dim), BF16),
            pltpu.VMEM((2, rows, head_dim), BF16),
            pltpu.VMEM((2, 128, head_dim), BF16),
            pltpu.VMEM((2 * head_dim, 128), BF16),
            pltpu.VMEM((heads, 8, rows), F32),
            pltpu.VMEM((heads, 8, rows), F32),
            pltpu.SemaphoreType.DMA((2, 2, 8)),
            pltpu.SemaphoreType.DMA((2, 2, 8)),
            pltpu.SemaphoreType.DMA((2, 2, 8)),
            pltpu.SemaphoreType.DMA((2, 2, 8)),
            pltpu.SemaphoreType.DMA((3, heads)),
            pltpu.SemaphoreType.DMA((4,)),
            pltpu.SemaphoreType.DMA((heads,)),
        ],
        compiler_params=pltpu.CompilerParams(
            collective_id=0, has_side_effects=True, vmem_limit_bytes=48 * 1024 * 1024
        ),
    )(queries, resp_keys, resp_values, prompt_keys, prompt_values, outputs, out_grads, lengths)


def solution(mesh):
    spec = P(("grp", "seq"), "kv")
    return jax.shard_map(
        functools.partial(per_device, mesh.shape["seq"]),
        mesh=mesh,
        in_specs=(spec,) * 7 + (P(("grp", "seq")),),
        out_specs=(spec,) * 5,
        check_vma=False,
    )
```

```python
import functools

import jax
import jax.numpy as jnp
from jax import lax
from jax.experimental import pallas as pl
from jax.experimental.pallas import tpu as pltpu
from jax.sharding import PartitionSpec as P

MESH = pl.DeviceIdType.MESH
F32 = jnp.float32
BF16 = jnp.bfloat16
LOG2E = 1.4426950408889634
LOW = -1e30
PARENT = {1: 0, 2: 0, 3: 2, 4: 2, 5: 4, 6: 4, 7: 6, 8: 6}
ROUNDS = (
    (">k2,k1,v2",),
    ("k2>k4,k3", "v2>v4,v1", "k1"),
    ("k4>k6,k5", "v4>v6,v3", "k3"),
    ("k6>k8,k7", "v6>v8,v7,v5", "k5"),
    ("k8", "k7"),
)
PLAN = (
    ("v8", "v7"),
    ("k8", "k7"),
    ("v5", "v6"),
    ("k5", "k6"),
    ("v3", "v4"),
    ("k3", "k4"),
    ("v1", "v2"),
    ("k1", "k2"),
    (),
    (),
)
HU = 8


def dot(a, b):
    return jnp.dot(a, b, preferred_element_type=F32)


def split3(x):
    hi = x.astype(BF16).astype(F32)
    mid = (x - hi).astype(BF16).astype(F32)
    lo = ((x - hi) - mid).astype(BF16).astype(F32)
    row = lax.broadcasted_iota(jnp.int32, (16, x.shape[1]), 0)
    out = jnp.where(row == 0, hi, jnp.where(row == 1, mid, jnp.where(row == 2, lo, 0.0)))
    return out.astype(BF16)


def kernel(
    n, heads, scale,
    q_hbm, kr_hbm, vr_hbm, kp_hbm, vp_hbm, o_hbm, g_hbm, len_ref,
    dq_out, dkr_out, dvr_out, dkp_out, dvp_out,
    kv, q3, g3, o3, qt, gt, kt, pd, part, sums, got, ext, m8, l8,
    ag_send, ag_recv, rs_send, rs_recv, in_sem, kv_sem,
):
    c2 = scale * LOG2E
    rows = q3.shape[1]
    head_dim = q3.shape[2]
    chunk = 2 * head_dim
    me = lax.axis_index("seq")

    def at(step):
        return {"seq": lax.rem(me + step + n, n)}

    barrier = pltpu.get_barrier_semaphore()
    for step in (1, -1, 2, -2):
        pl.semaphore_signal(barrier, inc=1, device_id=at(step), device_id_type=MESH)

    own = 8 * chunk
    local = [
        pltpu.make_async_copy(kp_hbm, kv.at[0, pl.ds(own, 128)], kv_sem.at[0]),
        pltpu.make_async_copy(vp_hbm, kv.at[1, pl.ds(own, 128)], kv_sem.at[1]),
        pltpu.make_async_copy(kr_hbm, kv.at[0, pl.ds(0, chunk)], kv_sem.at[2]),
        pltpu.make_async_copy(vr_hbm, kv.at[1, pl.ds(0, chunk)], kv_sem.at[3]),
    ]
    for copy in local:
        copy.start()
    loads = []
    for h in range(heads):
        for a, (src, dst) in enumerate(((q_hbm, q3), (g_hbm, g3), (o_hbm, o3))):
            copy = pltpu.make_async_copy(
                src.at[:, pl.ds(h * head_dim, head_dim)], dst.at[h], in_sem.at[a, h]
            )
            copy.start()
            loads.append(copy)

    def slot(d, way):
        if d == 8:
            return pl.ds(own + 128 + 64 * way, 64)
        return pl.ds(d * chunk + 128 * way, 128)

    def gather(kind, d, way):
        pa = PARENT[d]
        step = (d - pa) * (1 if way == 0 else -1)
        if pa == 0:
            src = (kp_hbm, vp_hbm)[kind]
        elif d == 8:
            src = kv.at[kind, pl.ds(pa * chunk + 128 * way + 64 * way, 64)]
        else:
            src = kv.at[kind, slot(pa, way)]
        return pltpu.make_async_remote_copy(
            src_ref=src, dst_ref=kv.at[kind, slot(d, way)],
            send_sem=ag_send.at[kind, way, d - 1], recv_sem=ag_recv.at[kind, way, d - 1],
            device_id=at(step), device_id_type=MESH,
        )

    def arrive(kind, d):
        for way in range(2):
            gather(kind, d, way).wait_recv()

    pl.semaphore_wait(barrier, 4)

    def run_round(i):
        for item in ROUNDS[i]:
            here, _, there = item.partition(">")
            if here:
                arrive("kv".index(here[0]), int(here[1]))
            for name in there.split(","):
                for way in range(2):
                    if name:
                        gather("kv".index(name[0]), int(name[1]), way).start()

    run_round(0)

    lane = lax.broadcasted_iota(jnp.int32, (chunk, 128), 1)
    ext[...] = jnp.where(lane < 3, -1.0, 0.0).astype(BF16)
    qt[pl.ds(head_dim, 128), :] = jnp.zeros((128, qt.shape[1]), BF16)
    gt[pl.ds(head_dim, 128), :] = jnp.zeros((128, gt.shape[1]), BF16)
    m8[...] = jnp.full(m8.shape, LOW, F32)
    l8[...] = jnp.zeros(l8.shape, F32)
    length = len_ref[0]
    live = lax.broadcasted_iota(jnp.int32, (rows, head_dim), 0) < length

    def cols(h):
        if isinstance(h, int):
            return pl.ds(h * rows, rows)
        return pl.ds(pl.multiple_of(h * rows, rows), rows)

    def prepare(h):
        g = jnp.where(live, g3[h].astype(F32), 0.0)
        o = o3[h].astype(F32)
        g3[h] = g.astype(BF16)
        g_t = g.T
        delta = jnp.sum(g_t * o.T, axis=0, keepdims=True)
        gt[pl.ds(0, head_dim), cols(h)] = g_t.astype(BF16)
        gt[pl.ds(head_dim, 16), cols(h)] = split3(delta)

    for h in range(heads):
        loads[3 * h].wait()
        qt[pl.ds(0, head_dim), cols(h)] = q3[h].astype(F32).T.astype(BF16)

    def causal():
        key = lax.broadcasted_iota(jnp.int32, (chunk, rows), 0)
        token = lax.broadcasted_iota(jnp.int32, (chunk, rows), 1)
        return key <= token

    def chunk_rows(c):
        if isinstance(c, int):
            return pl.ds(c * chunk, chunk)
        return pl.ds(pl.multiple_of(c * chunk, chunk), chunk)

    def first_pass(c, w=1, masked=False):
        keys = kv[0, pl.ds(c * chunk, w * chunk)]
        for h in range(heads):
            s = dot(keys, qt[pl.ds(0, head_dim), cols(h)])
            if masked:
                s = jnp.where(causal(), s, LOW)
            s = s.reshape(w * chunk // 8, 8, rows)
            old = m8[h]
            new = jnp.maximum(old, jnp.max(s, axis=0))
            e = jnp.exp2((s - new[None]) * c2)
            l8[h] = l8[h] * jnp.exp2((old - new) * c2) + jnp.sum(e, axis=0)
            m8[h] = new

    def turn(c):
        kt[:, chunk_rows(c)] = kv[0, chunk_rows(c)].astype(F32).T.astype(BF16)

    def finish_first():
        def step(h, carry):
            m = jnp.max(m8[h], axis=0, keepdims=True)
            total = jnp.sum(l8[h] * jnp.exp2((m8[h] - m) * c2), axis=0, keepdims=True)
            lse = m + jnp.log(total) * (1.0 / scale)
            qt[pl.ds(head_dim, 16), cols(h)] = split3(lse)
            return carry

        lax.fori_loop(0, heads, step, 0, unroll=HU)

    def probs(c, w=1, masked=False):
        r = pl.ds(c * chunk, chunk * w)
        keys = jnp.concatenate([kv[0, r], jnp.concatenate([ext[...]] * w, axis=0)], axis=1)
        for h in range(heads):
            p = jnp.exp2(dot(keys, qt[:, cols(h)]) * c2)
            if masked:
                p = jnp.where(causal(), p, 0.0)
            pd[r, cols(h)] = p.astype(BF16)
        part[1, r] = dot(pd[r, :], g3[...].reshape(heads * rows, head_dim))

    def dscores(c, w=1):
        r = pl.ds(c * chunk, chunk * w)
        values = jnp.concatenate([kv[1, r], jnp.concatenate([ext[...]] * w, axis=0)], axis=1)
        for h in range(heads):
            dp = dot(values, gt[:, cols(h)])
            pd[r, cols(h)] = (pd[r, cols(h)].astype(F32) * dp).astype(BF16)
        part[0, r] = dot(pd[r, :], q3[...].reshape(heads * rows, head_dim))

    local[2].wait()
    local[3].wait()
    local[0].wait()
    local[1].wait()

    def pair(hi, body):
        def step(i, carry):
            body(hi - i)
            return carry

        lax.fori_loop(0, 2, step, 0)

    for i in (1, 2, 3, 4):
        run_round(i)
        if i == 1:
            first_pass(0, masked=True)
        if i == 2:
            for copy in loads[1::3] + loads[2::3]:
                copy.wait()
            for h in range(heads):
                prepare(h)
        first_pass(2 * i - 1, 2)
        if i < 4:
            pair(2 * i, turn)
    finish_first()

    factor = (scale, 1.0)

    def mine(kind, d, way):
        if d == 0:
            r = pl.ds(own, 128)
        elif d == 8:
            r = pl.ds(own + 128 + 64 * way, 64)
        else:
            r = pl.ds(d * chunk + 128 * (1 - way), 128)
        return part[kind, r] * factor[kind]

    def rs_rows(d, way):
        return pl.ds(64 * way, 64) if d == 8 else pl.ds(0, 128)

    def scatter(kind, d, way):
        step = (d - PARENT[d]) * (1 if way == 0 else -1)
        r = rs_rows(d, way)
        return pltpu.make_async_remote_copy(
            src_ref=sums.at[kind, way, d - 1, r], dst_ref=got.at[kind, way, d - 1, r],
            send_sem=rs_send.at[kind, way, d - 1], recv_sem=rs_recv.at[kind, way, d - 1],
            device_id=at(step), device_id_type=MESH,
        )

    def total(kind, d, way, acc):
        for child in (8, 7, 6, 5, 4, 3, 2, 1):
            if PARENT[child] != d:
                continue
            scatter(kind, child, way).wait_recv()
            term = got[kind, way, child - 1, rs_rows(child, way)].astype(F32)
            if child == 8:
                if way == 0:
                    acc = jnp.concatenate([acc[:64] + term, acc[64:]], axis=0)
                else:
                    acc = jnp.concatenate([acc[:64], acc[64:] + term], axis=0)
            else:
                acc = acc + term
        return acc

    def send_sum(kind, d):
        for way in range(2):
            acc = total(kind, d, way, mine(kind, d, way))
            sums[kind, way, d - 1, rs_rows(d, way)] = acc.astype(BF16)
            scatter(kind, d, way).start()

    def last_values():
        for d in (1, 3, 5, 8, 7):
            arrive(1, d)

    steps = (
        lambda: probs(7, 2),
        lambda: (last_values(), dscores(7, 2)),
        lambda: probs(5, 2),
        lambda: dscores(5, 2),
        lambda: probs(3, 2),
        lambda: dscores(3, 2),
        lambda: probs(1, 2),
        lambda: dscores(1, 2),
        lambda: probs(0, masked=True),
        lambda: (pair(8, turn), turn(0), dscores(0)),
    )
    for i, step in enumerate(steps):
        step()
        for name in PLAN[i]:
            send_sum("kv".index(name[0]), int(name[1]))

    dkr_out[...] = (part[0, pl.ds(0, chunk)] * scale).astype(BF16)
    dvr_out[...] = part[1, pl.ds(0, chunk)].astype(BF16)
    for h in range(heads):
        d_q = dot(kt[...], pd[:, cols(h)]) * scale
        dq_out[:, pl.ds(h * head_dim, head_dim)] = d_q.T.astype(BF16)

    for kind in (1, 0):
        acc = mine(kind, 0, 0)
        for way in range(2):
            acc = total(kind, 0, way, acc)
        (dkp_out, dvp_out)[kind][...] = acc.astype(BF16)

    for kind in range(2):
        for d in range(1, 9):
            for way in range(2):
                gather(kind, d, way).wait_send()
                scatter(kind, d, way).wait_send()


def deliver(*refs):
    copies = [pltpu.make_async_copy(refs[i], refs[5 + i], refs[10].at[i]) for i in range(5)]
    for copy in copies:
        copy.start()
    for copy in copies:
        copy.wait()


def per_device(n, queries, resp_keys, resp_values, prompt_keys, prompt_values, outputs, out_grads, lengths):
    rows = queries.shape[0]
    head_dim = resp_keys.shape[1]
    heads = queries.shape[1] // head_dim
    scale = head_dim ** (-0.5)
    keys = n * prompt_keys.shape[0] + rows
    wide = heads * rows
    any_spec = pl.BlockSpec(memory_space=pl.ANY)
    vmem_spec = pl.BlockSpec(memory_space=pltpu.VMEM)
    outs = (queries, resp_keys, resp_values, prompt_keys, prompt_values)
    inputs = tuple(
        pltpu.with_memory_space_constraint(x, pltpu.HBM) for x in outs + (outputs, out_grads)
    )
    results = pl.pallas_call(
        functools.partial(kernel, n, heads, scale),
        out_shape=tuple(pltpu.VMEM(x.shape, BF16) for x in outs),
        in_specs=[any_spec] * 7 + [pl.BlockSpec(memory_space=pltpu.SMEM)],
        out_specs=(vmem_spec,) * 5,
        scratch_shapes=[
            pltpu.VMEM((2, keys, head_dim), BF16),
            pltpu.VMEM((heads, rows, head_dim), BF16),
            pltpu.VMEM((heads, rows, head_dim), BF16),
            pltpu.VMEM((heads, rows, head_dim), BF16),
            pltpu.VMEM((2 * head_dim, wide), BF16),
            pltpu.VMEM((2 * head_dim, wide), BF16),
            pltpu.VMEM((head_dim, keys), BF16),
            pltpu.VMEM((keys, wide), BF16),
            pltpu.VMEM((2, keys, head_dim), F32),
            pltpu.VMEM((2, 2, 8, 128, head_dim), BF16),
            pltpu.VMEM((2, 2, 8, 128, head_dim), BF16),
            pltpu.VMEM((2 * head_dim, 128), BF16),
            pltpu.VMEM((heads, 8, rows), F32),
            pltpu.VMEM((heads, 8, rows), F32),
            pltpu.SemaphoreType.DMA((2, 2, 8)),
            pltpu.SemaphoreType.DMA((2, 2, 8)),
            pltpu.SemaphoreType.DMA((2, 2, 8)),
            pltpu.SemaphoreType.DMA((2, 2, 8)),
            pltpu.SemaphoreType.DMA((3, heads)),
            pltpu.SemaphoreType.DMA((4,)),
        ],
        compiler_params=pltpu.CompilerParams(
            collective_id=0, has_side_effects=True, vmem_limit_bytes=44 * 1024 * 1024
        ),
    )(*inputs, lengths)
    return pl.pallas_call(
        deliver,
        out_shape=tuple(pltpu.HBM(x.shape, BF16) for x in outs),
        in_specs=[vmem_spec] * 5,
        out_specs=(any_spec,) * 5,
        scratch_shapes=[pltpu.SemaphoreType.DMA((5,))],
    )(*(pltpu.with_memory_space_constraint(x, pltpu.VMEM) for x in results))


def solution(mesh):
    spec = P(("grp", "seq"), "kv")
    return jax.shard_map(
        functools.partial(per_device, mesh.shape["seq"]),
        mesh=mesh,
        in_specs=(spec,) * 7 + (P(("grp", "seq")),),
        out_specs=(spec,) * 5,
        check_vma=False,
    )
```

```python
import functools

import jax
import jax.numpy as jnp
from jax import lax
from jax.experimental import pallas as pl
from jax.experimental.pallas import tpu as pltpu
from jax.sharding import PartitionSpec as P

MESH = pl.DeviceIdType.MESH
F32 = jnp.float32
BF16 = jnp.bfloat16
LOG2E = 1.4426950408889634
LOW = -1e30
PARENT = {1: 0, 2: 0, 3: 2, 4: 2, 5: 4, 6: 4, 7: 6, 8: 6}
ROUNDS = (
    (">k2,k1,v2",),
    ("k2>k4,k3", "v2>v4,v1", "k1"),
    ("k4>k6,k5", "v4>v6,v3", "k3"),
    ("k6>k8,k7", "v6>v8,v7,v5", "k5"),
    ("k8", "k7"),
)
PLAN = (
    ("v8", "v7"),
    ("k8", "k7"),
    ("v5", "v6"),
    ("k5", "k6"),
    ("v3", "v4"),
    ("k3", "k4"),
    ("v1", "v2"),
    ("k1", "k2"),
    (),
    (),
)
HU = 8


def dot(a, b):
    return jnp.dot(a, b, preferred_element_type=F32)


def split3(x):
    hi = x.astype(BF16).astype(F32)
    mid = (x - hi).astype(BF16).astype(F32)
    lo = ((x - hi) - mid).astype(BF16).astype(F32)
    row = lax.broadcasted_iota(jnp.int32, (16, x.shape[1]), 0)
    out = jnp.where(row == 0, hi, jnp.where(row == 1, mid, jnp.where(row == 2, lo, 0.0)))
    return out.astype(BF16)


def kernel(
    n, heads, scale,
    q_hbm, kr_hbm, vr_hbm, kp_hbm, vp_hbm, o_hbm, g_hbm, len_ref,
    dq_out, dkr_out, dvr_out, dkp_out, dvp_out,
    kv, q3, g3, o3, qt, gt, kt, pd, part, sums, got, ext, m8, l8,
    ag_send, ag_recv, rs_send, rs_recv, in_sem, kv_sem,
):
    c2 = scale * LOG2E
    rows = q3.shape[1]
    head_dim = q3.shape[2]
    chunk = 2 * head_dim
    me = lax.axis_index("seq")

    def at(step):
        return {"seq": lax.rem(me + step + n, n)}

    barrier = pltpu.get_barrier_semaphore()
    for step in (1, -1, 2, -2):
        pl.semaphore_signal(barrier, inc=1, device_id=at(step), device_id_type=MESH)

    own = chunk
    near = own + 128

    def first(d):
        return near + (d - 1) * chunk

    def slot(d, way):
        if d == 8:
            return pl.ds(first(d) + 64 * way, 64)
        return pl.ds(first(d) + 128 * way, 128)

    def gather(kind, d, way):
        pa = PARENT[d]
        step = (d - pa) * (1 if way == 0 else -1)
        if pa == 0:
            src = (kp_hbm, vp_hbm)[kind]
        elif d == 8:
            src = kv.at[kind, pl.ds(first(pa) + 128 * way + 64 * way, 64)]
        else:
            src = kv.at[kind, slot(pa, way)]
        return pltpu.make_async_remote_copy(
            src_ref=src, dst_ref=kv.at[kind, slot(d, way)],
            send_sem=ag_send.at[kind, way, d - 1], recv_sem=ag_recv.at[kind, way, d - 1],
            device_id=at(step), device_id_type=MESH,
        )

    def arrive(kind, d):
        for way in range(2):
            gather(kind, d, way).wait_recv()

    pl.semaphore_wait(barrier, 4)

    def run_round(i):
        for item in ROUNDS[i]:
            here, _, there = item.partition(">")
            if here:
                arrive("kv".index(here[0]), int(here[1]))
            for name in there.split(","):
                for way in range(2):
                    if name:
                        gather("kv".index(name[0]), int(name[1]), way).start()

    run_round(0)

    local = [
        pltpu.make_async_copy(kp_hbm, kv.at[0, pl.ds(own, 128)], kv_sem.at[0]),
        pltpu.make_async_copy(vp_hbm, kv.at[1, pl.ds(own, 128)], kv_sem.at[1]),
        pltpu.make_async_copy(kr_hbm, kv.at[0, pl.ds(0, chunk)], kv_sem.at[2]),
        pltpu.make_async_copy(vr_hbm, kv.at[1, pl.ds(0, chunk)], kv_sem.at[3]),
    ]
    for copy in local:
        copy.start()
    loads = []
    for h in range(heads):
        for a, (src, dst) in enumerate(((q_hbm, q3), (g_hbm, g3), (o_hbm, o3))):
            copy = pltpu.make_async_copy(
                src.at[:, pl.ds(h * head_dim, head_dim)], dst.at[h], in_sem.at[a, h]
            )
            copy.start()
            loads.append(copy)

    lane = lax.broadcasted_iota(jnp.int32, ext.shape, 1)
    ext[...] = jnp.where(lane < 3, -1.0, 0.0).astype(BF16)
    qt[pl.ds(head_dim, 128), :] = jnp.zeros((128, qt.shape[1]), BF16)
    gt[pl.ds(head_dim, 128), :] = jnp.zeros((128, gt.shape[1]), BF16)
    m8[...] = jnp.full(m8.shape, LOW, F32)
    l8[...] = jnp.zeros(l8.shape, F32)
    length = len_ref[0]
    live = lax.broadcasted_iota(jnp.int32, (rows, head_dim), 0) < length

    def cols(h):
        if isinstance(h, int):
            return pl.ds(h * rows, rows)
        return pl.ds(pl.multiple_of(h * rows, rows), rows)

    def prepare(h):
        g = jnp.where(live, g3[h].astype(F32), 0.0)
        o = o3[h].astype(F32)
        g3[h] = g.astype(BF16)
        g_t = g.T
        delta = jnp.sum(g_t * o.T, axis=0, keepdims=True)
        gt[pl.ds(0, head_dim), cols(h)] = g_t.astype(BF16)
        gt[pl.ds(head_dim, 16), cols(h)] = split3(delta)

    for h in range(heads):
        loads[3 * h].wait()
        qt[pl.ds(0, head_dim), cols(h)] = q3[h].astype(F32).T.astype(BF16)

    def allowed():
        key = lax.broadcasted_iota(jnp.int32, (near, rows), 0)
        token = lax.broadcasted_iota(jnp.int32, (near, rows), 1)
        return jnp.logical_or(key <= token, key >= chunk)

    def first_pass(start, size, masked=False):
        keys = kv[0, pl.ds(start, size)]
        for h in range(heads):
            s = dot(keys, qt[pl.ds(0, head_dim), cols(h)])
            if masked:
                s = jnp.where(allowed(), s, LOW)
            s = s.reshape(size // 8, 8, rows)
            old = m8[h]
            new = jnp.maximum(old, jnp.max(s, axis=0))
            e = jnp.exp2((s - new[None]) * c2)
            l8[h] = l8[h] * jnp.exp2((old - new) * c2) + jnp.sum(e, axis=0)
            m8[h] = new

    def turn(start, size):
        r = pl.ds(start, size)
        kt[:, r] = kv[0, r].astype(F32).T.astype(BF16)

    def finish_first():
        def step(h, carry):
            m = jnp.max(m8[h], axis=0, keepdims=True)
            total = jnp.sum(l8[h] * jnp.exp2((m8[h] - m) * c2), axis=0, keepdims=True)
            lse = m + jnp.log(total) * (1.0 / scale)
            qt[pl.ds(head_dim, 16), cols(h)] = split3(lse)
            return carry

        lax.fori_loop(0, heads, step, 0, unroll=HU)

    def probs(start, size, masked=False):
        r = pl.ds(start, size)
        keys = jnp.concatenate([kv[0, r], ext[pl.ds(0, size)]], axis=1)
        for h in range(heads):
            p = jnp.exp2(dot(keys, qt[:, cols(h)]) * c2)
            if masked:
                p = jnp.where(allowed(), p, 0.0)
            pd[r, cols(h)] = p.astype(BF16)
        part[1, r] = dot(pd[r, :], g3[...].reshape(heads * rows, head_dim))

    def dscores(start, size):
        r = pl.ds(start, size)
        values = jnp.concatenate([kv[1, r], ext[pl.ds(0, size)]], axis=1)
        for h in range(heads):
            dp = dot(values, gt[:, cols(h)])
            pd[r, cols(h)] = (pd[r, cols(h)].astype(F32) * dp).astype(BF16)
        part[0, r] = dot(pd[r, :], q3[...].reshape(heads * rows, head_dim))

    for copy in local:
        copy.wait()

    pairs = ((first(1), 2 * chunk), (first(3), 2 * chunk), (first(5), 2 * chunk), (first(7), chunk + 128))
    for i in (1, 2, 3, 4):
        run_round(i)
        if i == 1:
            first_pass(0, near, masked=True)
            turn(0, near)
        if i == 2:
            for copy in loads[1::3] + loads[2::3]:
                copy.wait()
            for h in range(heads):
                prepare(h)
        first_pass(*pairs[i - 1])
        if i < 4:
            turn(*pairs[i - 1])
    finish_first()

    factor = (scale, 1.0)

    def mine(kind, d, way):
        if d == 0:
            r = pl.ds(own, 128)
        elif d == 8:
            r = pl.ds(first(d) + 64 * way, 64)
        else:
            r = pl.ds(first(d) + 128 * (1 - way), 128)
        return part[kind, r] * factor[kind]

    def rs_rows(d, way):
        return pl.ds(64 * way, 64) if d == 8 else pl.ds(0, 128)

    def scatter(kind, d, way):
        step = (d - PARENT[d]) * (1 if way == 0 else -1)
        r = rs_rows(d, way)
        return pltpu.make_async_remote_copy(
            src_ref=sums.at[kind, way, d - 1, r], dst_ref=got.at[kind, way, d - 1, r],
            send_sem=rs_send.at[kind, way, d - 1], recv_sem=rs_recv.at[kind, way, d - 1],
            device_id=at(step), device_id_type=MESH,
        )

    def total(kind, d, way, acc):
        for child in (8, 7, 6, 5, 4, 3, 2, 1):
            if PARENT[child] != d:
                continue
            scatter(kind, child, way).wait_recv()
            term = got[kind, way, child - 1, rs_rows(child, way)].astype(F32)
            if child == 8:
                if way == 0:
                    acc = jnp.concatenate([acc[:64] + term, acc[64:]], axis=0)
                else:
                    acc = jnp.concatenate([acc[:64], acc[64:] + term], axis=0)
            else:
                acc = acc + term
        return acc

    def send_sum(kind, d):
        for way in range(2):
            acc = total(kind, d, way, mine(kind, d, way))
            sums[kind, way, d - 1, rs_rows(d, way)] = acc.astype(BF16)
            scatter(kind, d, way).start()

    def last_values():
        for d in (1, 3, 5, 8, 7):
            arrive(1, d)

    steps = (
        lambda: probs(*pairs[3]),
        lambda: (last_values(), dscores(*pairs[3])),
        lambda: probs(*pairs[2]),
        lambda: dscores(*pairs[2]),
        lambda: probs(*pairs[1]),
        lambda: dscores(*pairs[1]),
        lambda: probs(*pairs[0]),
        lambda: dscores(*pairs[0]),
        lambda: probs(0, near, masked=True),
        lambda: (dscores(0, near), turn(*pairs[3])),
    )
    for i, step in enumerate(steps):
        step()
        for name in PLAN[i]:
            send_sum("kv".index(name[0]), int(name[1]))

    dkr_out[...] = (part[0, pl.ds(0, chunk)] * scale).astype(BF16)
    dvr_out[...] = part[1, pl.ds(0, chunk)].astype(BF16)
    for h in range(heads):
        d_q = dot(kt[...], pd[:, cols(h)]) * scale
        dq_out[:, pl.ds(h * head_dim, head_dim)] = d_q.T.astype(BF16)

    for kind in (1, 0):
        acc = mine(kind, 0, 0)
        for way in range(2):
            acc = total(kind, 0, way, acc)
        (dkp_out, dvp_out)[kind][...] = acc.astype(BF16)

    for kind in range(2):
        for d in range(1, 9):
            for way in range(2):
                gather(kind, d, way).wait_send()
                scatter(kind, d, way).wait_send()


def deliver(*refs):
    copies = [pltpu.make_async_copy(refs[i], refs[5 + i], refs[10].at[i]) for i in range(5)]
    for copy in copies:
        copy.start()
    for copy in copies:
        copy.wait()


def per_device(n, queries, resp_keys, resp_values, prompt_keys, prompt_values, outputs, out_grads, lengths):
    rows = queries.shape[0]
    head_dim = resp_keys.shape[1]
    heads = queries.shape[1] // head_dim
    scale = head_dim ** (-0.5)
    keys = n * prompt_keys.shape[0] + rows
    wide = heads * rows
    any_spec = pl.BlockSpec(memory_space=pl.ANY)
    vmem_spec = pl.BlockSpec(memory_space=pltpu.VMEM)
    outs = (queries, resp_keys, resp_values, prompt_keys, prompt_values)
    inputs = tuple(
        pltpu.with_memory_space_constraint(x, pltpu.HBM) for x in outs + (outputs, out_grads)
    )
    results = pl.pallas_call(
        functools.partial(kernel, n, heads, scale),
        out_shape=tuple(pltpu.VMEM(x.shape, BF16) for x in outs),
        in_specs=[any_spec] * 7 + [pl.BlockSpec(memory_space=pltpu.SMEM)],
        out_specs=(vmem_spec,) * 5,
        scratch_shapes=[
            pltpu.VMEM((2, keys, head_dim), BF16),
            pltpu.VMEM((heads, rows, head_dim), BF16),
            pltpu.VMEM((heads, rows, head_dim), BF16),
            pltpu.VMEM((heads, rows, head_dim), BF16),
            pltpu.VMEM((2 * head_dim, wide), BF16),
            pltpu.VMEM((2 * head_dim, wide), BF16),
            pltpu.VMEM((head_dim, keys), BF16),
            pltpu.VMEM((keys, wide), BF16),
            pltpu.VMEM((2, keys, head_dim), F32),
            pltpu.VMEM((2, 2, 8, 128, head_dim), BF16),
            pltpu.VMEM((2, 2, 8, 128, head_dim), BF16),
            pltpu.VMEM((4 * head_dim, 128), BF16),
            pltpu.VMEM((heads, 8, rows), F32),
            pltpu.VMEM((heads, 8, rows), F32),
            pltpu.SemaphoreType.DMA((2, 2, 8)),
            pltpu.SemaphoreType.DMA((2, 2, 8)),
            pltpu.SemaphoreType.DMA((2, 2, 8)),
            pltpu.SemaphoreType.DMA((2, 2, 8)),
            pltpu.SemaphoreType.DMA((3, heads)),
            pltpu.SemaphoreType.DMA((4,)),
        ],
        compiler_params=pltpu.CompilerParams(
            collective_id=0, has_side_effects=True, vmem_limit_bytes=44 * 1024 * 1024
        ),
    )(*inputs, lengths)
    return pl.pallas_call(
        deliver,
        out_shape=tuple(pltpu.HBM(x.shape, BF16) for x in outs),
        in_specs=[vmem_spec] * 5,
        out_specs=(any_spec,) * 5,
        scratch_shapes=[pltpu.SemaphoreType.DMA((5,))],
    )(*(pltpu.with_memory_space_constraint(x, pltpu.VMEM) for x in results))


def solution(mesh):
    spec = P(("grp", "seq"), "kv")
    return jax.shard_map(
        functools.partial(per_device, mesh.shape["seq"]),
        mesh=mesh,
        in_specs=(spec,) * 7 + (P(("grp", "seq")),),
        out_specs=(spec,) * 5,
        check_vma=False,
    )
```

```python
import functools

import jax
import jax.numpy as jnp
from jax import lax
from jax.experimental import pallas as pl
from jax.experimental.pallas import tpu as pltpu
from jax.sharding import PartitionSpec as P

MESH = pl.DeviceIdType.MESH
F32 = jnp.float32
BF16 = jnp.bfloat16
LOG2E = 1.4426950408889634
LOW = -1e30
PARENT = {1: 0, 2: 0, 3: 2, 4: 2, 5: 4, 6: 4, 7: 6, 8: 6}
ROUNDS = (
    (">k2,k1,v2",),
    ("k2>k4,k3", "v2>v4,v1", "k1"),
    ("k4>k6,k5", "v4>v6,v3", "k3"),
    ("k6>k8,k7", "v6>v8,v7,v5", "k5"),
    ("k8", "k7"),
)
PLAN = (
    ("v8", "v7"),
    ("k8", "k7"),
    ("v5", "v6"),
    ("k5", "k6"),
    ("v3", "v4"),
    ("k3", "k4"),
    ("v1", "v2"),
    ("k1", "k2"),
    (),
    (),
)
HU = 8


def dot(a, b):
    return jnp.dot(a, b, preferred_element_type=F32)


def split3(x):
    hi = x.astype(BF16).astype(F32)
    mid = (x - hi).astype(BF16).astype(F32)
    lo = ((x - hi) - mid).astype(BF16).astype(F32)
    row = lax.broadcasted_iota(jnp.int32, (16, x.shape[1]), 0)
    out = jnp.where(row == 0, hi, jnp.where(row == 1, mid, jnp.where(row == 2, lo, 0.0)))
    return out.astype(BF16)


def kernel(
    n, heads, scale,
    q_hbm, kr_hbm, vr_hbm, kp_hbm, vp_hbm, o_hbm, g_hbm, len_ref,
    dq_out, dkr_out, dvr_out, dkp_out, dvp_out,
    kv, q3, g3, o3, qt, gt, kt, pd, part, sums, got, ext, m8, l8,
    ag_send, ag_recv, rs_send, rs_recv, in_sem, kv_sem,
):
    c2 = scale * LOG2E
    rows = q3.shape[1]
    head_dim = q3.shape[2]
    chunk = 2 * head_dim
    me = lax.axis_index("seq")

    def at(step):
        return {"seq": lax.rem(me + step + n, n)}

    barrier = pltpu.get_barrier_semaphore()
    for step in (1, -1, 2, -2):
        pl.semaphore_signal(barrier, inc=1, device_id=at(step), device_id_type=MESH)

    own = chunk
    near = own + 128

    def first(d):
        return near + (d - 1) * chunk

    def slot(d, way):
        if d == 8:
            return pl.ds(first(d) + 64 * way, 64)
        return pl.ds(first(d) + 128 * way, 128)

    def gather(kind, d, way):
        pa = PARENT[d]
        step = (d - pa) * (1 if way == 0 else -1)
        if pa == 0:
            src = (kp_hbm, vp_hbm)[kind]
        elif d == 8:
            src = kv.at[kind, pl.ds(first(pa) + 128 * way + 64 * way, 64)]
        else:
            src = kv.at[kind, slot(pa, way)]
        return pltpu.make_async_remote_copy(
            src_ref=src, dst_ref=kv.at[kind, slot(d, way)],
            send_sem=ag_send.at[kind, way, d - 1], recv_sem=ag_recv.at[kind, way, d - 1],
            device_id=at(step), device_id_type=MESH,
        )

    def arrive(kind, d):
        for way in range(2):
            gather(kind, d, way).wait_recv()

    pl.semaphore_wait(barrier, 4)

    def run_round(i):
        for item in ROUNDS[i]:
            here, _, there = item.partition(">")
            if here:
                arrive("kv".index(here[0]), int(here[1]))
            for name in there.split(","):
                for way in range(2):
                    if name:
                        gather("kv".index(name[0]), int(name[1]), way).start()

    run_round(0)

    local = [
        pltpu.make_async_copy(kp_hbm, kv.at[0, pl.ds(own, 128)], kv_sem.at[0]),
        pltpu.make_async_copy(vp_hbm, kv.at[1, pl.ds(own, 128)], kv_sem.at[1]),
        pltpu.make_async_copy(kr_hbm, kv.at[0, pl.ds(0, chunk)], kv_sem.at[2]),
        pltpu.make_async_copy(vr_hbm, kv.at[1, pl.ds(0, chunk)], kv_sem.at[3]),
    ]
    for copy in local:
        copy.start()
    loads = []
    for h in range(heads):
        for a, (src, dst) in enumerate(((q_hbm, q3), (g_hbm, g3), (o_hbm, o3))):
            copy = pltpu.make_async_copy(
                src.at[:, pl.ds(h * head_dim, head_dim)], dst.at[h], in_sem.at[a, h]
            )
            copy.start()
            loads.append(copy)

    lane = lax.broadcasted_iota(jnp.int32, ext.shape, 1)
    ext[...] = jnp.where(lane < 3, -1.0, 0.0).astype(BF16)
    qt[pl.ds(head_dim, 128), :] = jnp.zeros((128, qt.shape[1]), BF16)
    gt[pl.ds(head_dim, 128), :] = jnp.zeros((128, gt.shape[1]), BF16)
    m8[...] = jnp.full(m8.shape, LOW, F32)
    l8[...] = jnp.zeros(l8.shape, F32)
    length = len_ref[0]
    live = lax.broadcasted_iota(jnp.int32, (rows, head_dim), 0) < length

    def cols(h):
        if isinstance(h, int):
            return pl.ds(h * rows, rows)
        return pl.ds(pl.multiple_of(h * rows, rows), rows)

    def prepare(h):
        g = jnp.where(live, g3[h].astype(F32), 0.0)
        o = o3[h].astype(F32)
        g3[h] = g.astype(BF16)
        g_t = g.T
        delta = jnp.sum(g_t * o.T, axis=0, keepdims=True)
        gt[pl.ds(0, head_dim), cols(h)] = g_t.astype(BF16)
        gt[pl.ds(head_dim, 16), cols(h)] = split3(delta)

    for h in range(heads):
        loads[3 * h].wait()
        qt[pl.ds(0, head_dim), cols(h)] = q3[h].astype(F32).T.astype(BF16)

    def allowed():
        key = lax.broadcasted_iota(jnp.int32, (near, rows), 0)
        token = lax.broadcasted_iota(jnp.int32, (near, rows), 1)
        return jnp.logical_or(key <= token, key >= chunk)

    def finish(h, peaks, sums_of):
        m = jnp.max(peaks, axis=0, keepdims=True)
        all_of = jnp.sum(sums_of * jnp.exp2((peaks - m) * c2), axis=0, keepdims=True)
        qt[pl.ds(head_dim, 16), cols(h)] = split3(m + jnp.log(all_of) * (1.0 / scale))

    def first_pass(start, size, masked=False, last=False):
        keys = kv[0, pl.ds(start, size)]
        for h in range(heads):
            s = dot(keys, qt[pl.ds(0, head_dim), cols(h)])
            if masked:
                s = jnp.where(allowed(), s, LOW)
            s = s.reshape(size // 8, 8, rows)
            old = m8[h]
            new = jnp.maximum(old, jnp.max(s, axis=0))
            e = jnp.exp2((s - new[None]) * c2)
            sums_of = l8[h] * jnp.exp2((old - new) * c2) + jnp.sum(e, axis=0)
            if last:
                finish(h, new, sums_of)
            else:
                l8[h] = sums_of
                m8[h] = new

    def turn(start, size):
        r = pl.ds(start, size)
        kt[:, r] = kv[0, r].astype(F32).T.astype(BF16)

    def probs(start, size, masked=False):
        r = pl.ds(start, size)
        keys = jnp.concatenate([kv[0, r], ext[pl.ds(0, size)]], axis=1)
        for h in range(heads):
            p = jnp.exp2(dot(keys, qt[:, cols(h)]) * c2)
            if masked:
                p = jnp.where(allowed(), p, 0.0)
            pd[r, cols(h)] = p.astype(BF16)
        part[1, r] = dot(pd[r, :], g3[...].reshape(heads * rows, head_dim))

    def dscores(start, size):
        r = pl.ds(start, size)
        values = jnp.concatenate([kv[1, r], ext[pl.ds(0, size)]], axis=1)
        for h in range(heads):
            dp = dot(values, gt[:, cols(h)])
            pd[r, cols(h)] = (pd[r, cols(h)].astype(F32) * dp).astype(BF16)
        part[0, r] = dot(pd[r, :], q3[...].reshape(heads * rows, head_dim))

    for copy in local:
        copy.wait()

    pairs = ((first(1), 2 * chunk), (first(3), 2 * chunk), (first(5), 2 * chunk), (first(7), chunk + 128))
    for i in (1, 2, 3, 4):
        run_round(i)
        if i == 1:
            first_pass(0, near, masked=True)
            turn(0, near)
        if i == 2:
            for copy in loads[1::3] + loads[2::3]:
                copy.wait()
            for h in range(heads):
                prepare(h)
        first_pass(*pairs[i - 1], last=i == 4)
        if i < 4:
            turn(*pairs[i - 1])

    factor = (scale, 1.0)

    def mine(kind, d, way):
        if d == 0:
            r = pl.ds(own, 128)
        elif d == 8:
            r = pl.ds(first(d) + 64 * way, 64)
        else:
            r = pl.ds(first(d) + 128 * (1 - way), 128)
        return part[kind, r] * factor[kind]

    def rs_rows(d, way):
        return pl.ds(64 * way, 64) if d == 8 else pl.ds(0, 128)

    def scatter(kind, d, way):
        step = (d - PARENT[d]) * (1 if way == 0 else -1)
        r = rs_rows(d, way)
        return pltpu.make_async_remote_copy(
            src_ref=sums.at[kind, way, d - 1, r], dst_ref=got.at[kind, way, d - 1, r],
            send_sem=rs_send.at[kind, way, d - 1], recv_sem=rs_recv.at[kind, way, d - 1],
            device_id=at(step), device_id_type=MESH,
        )

    def total(kind, d, way, acc):
        for child in (8, 7, 6, 5, 4, 3, 2, 1):
            if PARENT[child] != d:
                continue
            scatter(kind, child, way).wait_recv()
            term = got[kind, way, child - 1, rs_rows(child, way)].astype(F32)
            if child == 8:
                if way == 0:
                    acc = jnp.concatenate([acc[:64] + term, acc[64:]], axis=0)
                else:
                    acc = jnp.concatenate([acc[:64], acc[64:] + term], axis=0)
            else:
                acc = acc + term
        return acc

    def send_sum(kind, d):
        for way in range(2):
            acc = total(kind, d, way, mine(kind, d, way))
            sums[kind, way, d - 1, rs_rows(d, way)] = acc.astype(BF16)
            scatter(kind, d, way).start()

    def last_values():
        for d in (1, 3, 5, 8, 7):
            arrive(1, d)

    steps = (
        lambda: probs(*pairs[3]),
        lambda: (last_values(), dscores(*pairs[3])),
        lambda: probs(*pairs[2]),
        lambda: dscores(*pairs[2]),
        lambda: probs(*pairs[1]),
        lambda: dscores(*pairs[1]),
        lambda: probs(*pairs[0]),
        lambda: dscores(*pairs[0]),
        lambda: probs(0, near, masked=True),
        lambda: (dscores(0, near), turn(*pairs[3])),
    )
    for i, step in enumerate(steps):
        step()
        for name in PLAN[i]:
            send_sum("kv".index(name[0]), int(name[1]))

    dkr_out[...] = (part[0, pl.ds(0, chunk)] * scale).astype(BF16)
    dvr_out[...] = part[1, pl.ds(0, chunk)].astype(BF16)
    for h in range(heads):
        d_q = dot(kt[...], pd[:, cols(h)]) * scale
        dq_out[:, pl.ds(h * head_dim, head_dim)] = d_q.T.astype(BF16)

    for kind in (1, 0):
        acc = mine(kind, 0, 0)
        for way in range(2):
            acc = total(kind, 0, way, acc)
        (dkp_out, dvp_out)[kind][...] = acc.astype(BF16)

    for kind in range(2):
        for d in range(1, 9):
            for way in range(2):
                gather(kind, d, way).wait_send()
                scatter(kind, d, way).wait_send()


def deliver(*refs):
    copies = [pltpu.make_async_copy(refs[i], refs[5 + i], refs[10].at[i]) for i in range(1, 5)]
    part = refs[0].shape[0] // 4
    for i in range(4):
        r = pl.ds(i * part, part)
        sem = refs[10].at[0 if i == 0 else 4 + i]
        copies.insert(0, pltpu.make_async_copy(refs[0].at[r], refs[5].at[r], sem))
    for copy in copies:
        copy.start()
    for copy in copies:
        copy.wait()


def per_device(n, queries, resp_keys, resp_values, prompt_keys, prompt_values, outputs, out_grads, lengths):
    rows = queries.shape[0]
    head_dim = resp_keys.shape[1]
    heads = queries.shape[1] // head_dim
    scale = head_dim ** (-0.5)
    keys = n * prompt_keys.shape[0] + rows
    wide = heads * rows
    any_spec = pl.BlockSpec(memory_space=pl.ANY)
    vmem_spec = pl.BlockSpec(memory_space=pltpu.VMEM)
    outs = (queries, resp_keys, resp_values, prompt_keys, prompt_values)
    inputs = tuple(
        pltpu.with_memory_space_constraint(x, pltpu.HBM) for x in outs + (outputs, out_grads)
    )
    results = pl.pallas_call(
        functools.partial(kernel, n, heads, scale),
        out_shape=tuple(pltpu.VMEM(x.shape, BF16) for x in outs),
        in_specs=[any_spec] * 7 + [pl.BlockSpec(memory_space=pltpu.SMEM)],
        out_specs=(vmem_spec,) * 5,
        scratch_shapes=[
            pltpu.VMEM((2, keys, head_dim), BF16),
            pltpu.VMEM((heads, rows, head_dim), BF16),
            pltpu.VMEM((heads, rows, head_dim), BF16),
            pltpu.VMEM((heads, rows, head_dim), BF16),
            pltpu.VMEM((2 * head_dim, wide), BF16),
            pltpu.VMEM((2 * head_dim, wide), BF16),
            pltpu.VMEM((head_dim, keys), BF16),
            pltpu.VMEM((keys, wide), BF16),
            pltpu.VMEM((2, keys, head_dim), F32),
            pltpu.VMEM((2, 2, 8, 128, head_dim), BF16),
            pltpu.VMEM((2, 2, 8, 128, head_dim), BF16),
            pltpu.VMEM((4 * head_dim, 128), BF16),
            pltpu.VMEM((heads, 8, rows), F32),
            pltpu.VMEM((heads, 8, rows), F32),
            pltpu.SemaphoreType.DMA((2, 2, 8)),
            pltpu.SemaphoreType.DMA((2, 2, 8)),
            pltpu.SemaphoreType.DMA((2, 2, 8)),
            pltpu.SemaphoreType.DMA((2, 2, 8)),
            pltpu.SemaphoreType.DMA((3, heads)),
            pltpu.SemaphoreType.DMA((4,)),
        ],
        compiler_params=pltpu.CompilerParams(
            collective_id=0, has_side_effects=True, vmem_limit_bytes=44 * 1024 * 1024
        ),
    )(*inputs, lengths)
    return pl.pallas_call(
        deliver,
        out_shape=tuple(pltpu.HBM(x.shape, BF16) for x in outs),
        in_specs=[vmem_spec] * 5,
        out_specs=(any_spec,) * 5,
        scratch_shapes=[pltpu.SemaphoreType.DMA((8,))],
    )(*(pltpu.with_memory_space_constraint(x, pltpu.VMEM) for x in results))


def solution(mesh):
    spec = P(("grp", "seq"), "kv")
    return jax.shard_map(
        functools.partial(per_device, mesh.shape["seq"]),
        mesh=mesh,
        in_specs=(spec,) * 7 + (P(("grp", "seq")),),
        out_specs=(spec,) * 5,
        check_vma=False,
    )
```
